32 devices in a mesh: seq: 8 (over z, y), head: 4 (over x, core).
Axes of the slice: x: 2, y: 2, z: 4, core: 2. Of those that a mesh axis runs over, the one named last changes fastest.
Arguments:
- query: bfloat16 [5120, 2048], P(('seq', 'head')), may hold values from -5 to 5
- key: bfloat16 [5120, 2048], P(('seq', 'head')), may hold values from -5 to 5
- value: bfloat16 [5120, 2048], P(('seq', 'head')), may hold values from -6 to 6
- grad_out: bfloat16 [5120, 2048], P(('seq', 'head')), may hold values from -6 to 6
- rand_blocks: int32 [80, 3], replicated, may hold values from 0 to 79, as said below
Outputs:
- grad_query: bfloat16 [5120, 2048], P(('seq', 'head'))
- grad_key: bfloat16 [5120, 2048], P(('seq', 'head'))
- grad_value: bfloat16 [5120, 2048], P(('seq', 'head'))
The draws below stay inside these ranges and needn't reach their ends.
Inputs may be any that keep to these rules, and one draw needn't show every extreme that they name: `rand_blocks`: row j lists the 3 random key blocks of query block j. Block b lies on index b // 10 of seq. The blocks of one row lie on 3 different indices. No listed block lies on index 0 or on the index of the query block itself. The query blocks of one index of seq list at most 5 blocks lying on any one other index.
All inputs are finite; a program needn't handle non-finite values.
Results may differ from the reference program's by a relative error of at most 0.008.
Values may be sent and summed in bfloat16 or wider, within the bound.
A program may use at most 384 MiB of HBM per device.

```python
import jax
import jax.numpy as jnp
from jax import lax

H = 16
HD = 128
BLOCK = 64
G = 2
R = 3
BPD = 10
NB = 80
S = 5120


def base_values(key):
    return jnp.clip(jax.random.normal(key, (NB, BLOCK, H, HD)), -5.0, 5.0)


def draw_query(key, part):
    values_drawn = base_values(jax.random.fold_in(key, 1))
    return values_drawn.reshape(S, H * HD).astype(jnp.bfloat16)


def draw_key(key, part):
    values_drawn = base_values(jax.random.fold_in(key, 2))
    return values_drawn.reshape(S, H * HD).astype(jnp.bfloat16)


def draw_rand_blocks(key, part):
    seq_count = NB // BPD
    wanted = BPD * R
    devices = jnp.arange(seq_count, dtype=jnp.int32)

    def one_device(device, device_key):
        shuffle_key, within_key = jax.random.split(device_key)
        shuffled = jax.random.permutation(shuffle_key, seq_count).astype(jnp.int32)
        barred = (devices == 0) | (devices == device)
        ranked = jnp.argsort(shuffled + seq_count * barred.astype(jnp.int32)).astype(jnp.int32)
        eligible = seq_count - jnp.sum(barred.astype(jnp.int32))
        owners = ranked[jnp.arange(wanted, dtype=jnp.int32) % eligible]
        within = jax.random.randint(within_key, (wanted,), 0, BPD).astype(jnp.int32)
        return (owners * BPD + within).astype(jnp.int32)
    block_table = jax.vmap(one_device)(devices, jax.random.split(key, seq_count))
    return block_table.reshape(NB, R)


def shard_levels(key, extent, pieces, smallest, high):
    gain, own = 1.0, jax.random.fold_in(key, 6)
    for axis_at, blocks in pieces:
        heights = jnp.exp(jax.random.uniform(jax.random.fold_in(own, axis_at), (blocks,), jnp.float32, smallest / len(pieces), high / len(pieces)))
        gain = gain * jnp.repeat(heights, extent[axis_at] // blocks).reshape([-1 if axis == axis_at else 1 for axis in range(len(extent))])
    return gain


def gaussian(stream_key, dims, deviation, limit, pieces=(), held_as=jnp.bfloat16):
    gain = shard_levels(stream_key, dims, pieces, -0.22, 0.18) if pieces else 1.0
    values = jax.random.normal(stream_key, dims, jnp.float32) * deviation * gain
    return jnp.minimum(jnp.maximum(values, -limit), limit).astype(held_as)


def setup_inputs(seed: int = 0) -> dict:
    splits = jax.random.split(jax.random.key(seed), 6)
    query = draw_query(jax.random.fold_in(splits[5], 71), 0)
    key = draw_key(jax.random.fold_in(splits[5], 71), 0)
    value = gaussian(splits[2], (S, H * HD), 1.0, 6.0, ((0, 32),))
    grad_out = gaussian(splits[3], (S, H * HD), 1.0, 6.0, ((0, 32),))
    rand_blocks = draw_rand_blocks(jax.random.fold_in(splits[5], 71), 0)
    return dict(query=query, key=key, value=value, grad_out=grad_out, rand_blocks=rand_blocks)


big_negative = -1.0e30


def reference(query, key, value, grad_out, rand_blocks):
    score_scale = HD ** -0.5
    query_blocks = query.reshape(NB, BLOCK, H, HD)
    key_blocks = key.reshape(NB, BLOCK, H, HD)
    value_blocks = value.reshape(NB, BLOCK, H, HD)
    dout_blocks = grad_out.reshape(NB, BLOCK, H, HD)

    def visit_block(carry, block_index):
        key_sums, value_sums = carry
        glob_index = jnp.arange(G, dtype=jnp.int32)
        chosen = jnp.concatenate([jnp.stack([block_index - 1, block_index, block_index + 1]).astype(jnp.int32), glob_index, rand_blocks[block_index].astype(jnp.int32)])
        live_slots = jnp.concatenate([jnp.stack([block_index >= 1, block_index >= 0, block_index <= NB - 2]), jnp.abs(glob_index - block_index) > 1, jnp.ones((R,), jnp.bool_)])
        clamped = jnp.clip(chosen, 0, NB - 1).astype(jnp.int32)
        slot_keys = key_blocks[clamped].astype(jnp.float32)
        slot_values = value_blocks[clamped].astype(jnp.float32)
        rows_query = query_blocks[block_index].astype(jnp.float32)
        rows_dout = dout_blocks[block_index].astype(jnp.float32)
        scores = jnp.einsum("xhd,kyhd->hxky", rows_query, slot_keys) * score_scale
        scores = jnp.where(live_slots[None, None, :, None], scores, big_negative)
        row_max = jnp.max(scores, axis=(2, 3), keepdims=True)
        weights = jnp.exp(scores - row_max)
        probabilities = weights / jnp.sum(weights, axis=(2, 3), keepdims=True)
        prob_low = lax.optimization_barrier(probabilities.astype(jnp.bfloat16)).astype(jnp.float32)
        prob_grads = jnp.einsum("xhd,kyhd->hxky", rows_dout, slot_values)
        row_dot = jnp.sum(probabilities * prob_grads, axis=(2, 3), keepdims=True)
        score_grads = lax.optimization_barrier((probabilities * (prob_grads - row_dot)).astype(jnp.bfloat16)).astype(jnp.float32)
        query_grads = jnp.einsum("hxky,kyhd->xhd", score_grads, slot_keys) * score_scale
        key_terms = jnp.einsum("hxky,xhd->kyhd", score_grads, rows_query) * score_scale
        value_terms = jnp.einsum("hxky,xhd->kyhd", prob_low, rows_dout)
        key_sums = key_sums.at[clamped].add(key_terms)
        value_sums = value_sums.at[clamped].add(value_terms)
        return (key_sums, value_sums), query_grads.astype(jnp.bfloat16)

    empty_sums = jnp.zeros((NB, BLOCK, H, HD), jnp.float32)
    (key_sums, value_sums), query_grads = lax.scan(visit_block, (empty_sums, empty_sums), jnp.arange(NB, dtype=jnp.int32))
    return (query_grads.reshape(S, H * HD), key_sums.reshape(S, H * HD).astype(jnp.bfloat16), value_sums.reshape(S, H * HD).astype(jnp.bfloat16))
```

```python
import functools

import jax
import jax.numpy as jnp
from jax import lax
from jax.experimental import pallas as pl
from jax.experimental.pallas import tpu as pltpu
from jax.sharding import PartitionSpec as P

HD = 128
BLOCK = 64
G = 2
R = 3


big_negative = -1e30


def broadcast(block, axis, source):
    block = jnp.where(lax.axis_index(axis) == source, block, jnp.zeros_like(block))
    return lax.psum(block, axis)


def extended_2(shard, sides, width):
    for axis, dim in sides:
        peers, length = (lax.axis_size(axis), shard.shape[dim])
        up = [(i, (i + 1) % peers) for i in range(peers - 1)]
        down = [(j, i) for i, j in up]
        last = lax.slice_in_dim(shard, length - width, length, axis=dim)
        leading = lax.slice_in_dim(shard, 0, width, axis=dim)
        before = lax.ppermute(last, axis, up)
        after = lax.ppermute(leading, axis, down)
        shard = jnp.concatenate([before, shard, after], axis=dim)
    return shard


def request_plan(requested, device, per_dev):
    wanted_row = requested[device]
    owners = wanted_row // per_dev
    within = wanted_row % per_dev
    usable = jnp.ones(wanted_row.shape, jnp.bool_)
    positions = jnp.arange(owners.shape[0])
    earlier = (owners[:, None] == owners[None, :]) & (positions[None, :] < positions[:, None])
    slot_rank = jnp.sum(earlier.astype(jnp.int32), axis=1)
    return (owners, within, slot_rank, usable)


def on_device(query, key, value, grad_out, rand_blocks):
    queries, keys, values, out_grads = (
        lax.all_to_all(query, "head", split_axis=1, concat_axis=0, tiled=True),
        lax.all_to_all(key, "head", split_axis=1, concat_axis=0, tiled=True),
        lax.all_to_all(value, "head", split_axis=1, concat_axis=0, tiled=True),
        lax.all_to_all(grad_out, "head", split_axis=1, concat_axis=0, tiled=True),
    )
    tokens, features = queries.shape
    head_count = features // HD
    per_dev = tokens // BLOCK
    seq_count = lax.axis_size("seq")
    device = lax.axis_index("seq")
    capacity = (per_dev * R + seq_count - 3) // (seq_count - 2)
    rand_count = per_dev * R
    slots_total = 3 + G + R
    score_scale = HD ** (-0.5)
    requested = rand_blocks.reshape(seq_count, rand_count)
    owners_all, within_all, rank_all, usable_all = jax.vmap(
        lambda sender: request_plan(requested, sender, per_dev)
    )(jnp.arange(seq_count, dtype=jnp.int32))
    to_me = usable_all & (owners_all == device)
    slot_ids = jnp.arange(capacity)
    block_ids = jnp.arange(per_dev)
    matches = (
        to_me[:, :, None, None]
        & (rank_all[:, :, None, None] == slot_ids[None, None, :, None])
        & (within_all[:, :, None, None] == block_ids[None, None, None, :])
    )
    chooser = jnp.sum(matches.astype(jnp.float32), axis=1)
    my_owners, my_within, my_rank, my_usable = request_plan(requested, device, per_dev)
    my_slot = jnp.clip(my_owners, 0, seq_count - 1) * capacity + my_rank
    own_pairs = jnp.stack([keys, values]).reshape(2, per_dev, BLOCK, features)
    served = None
    served = jnp.einsum(
        "dcb,sbxf->dcsxf",
        chooser.astype(jnp.bfloat16),
        own_pairs,
        preferred_element_type=jnp.float32,
    ).astype(jnp.bfloat16)
    outgoing = served.reshape(seq_count * capacity, 2, BLOCK, features)
    incoming = lax.all_to_all(outgoing, "seq", split_axis=0, concat_axis=0, tiled=True)
    wanted = (my_slot[:, None] == jnp.arange(seq_count * capacity)[None, :]).astype(jnp.bfloat16)
    fetched = jnp.einsum(
        "ro,osxf->rsxf", wanted, incoming, preferred_element_type=jnp.float32
    ).astype(jnp.bfloat16)
    leading = jnp.stack([keys[: G * BLOCK], values[: G * BLOCK]])
    global_pairs = broadcast(leading, "seq", 0).reshape(2, G, BLOCK, features)
    extended = extended_2(jnp.stack([keys, values]), (("seq", 1),), BLOCK)
    left_pair = extended[:, :BLOCK]
    right_pair = extended[:, -BLOCK:]
    framed = jnp.concatenate([left_pair[:, None], own_pairs, right_pair[:, None]], axis=1)
    window = jnp.stack(
        [framed[:, 0:per_dev], framed[:, 1 : per_dev + 1], framed[:, 2 : per_dev + 2]], axis=2
    )
    global_slots = jnp.broadcast_to(global_pairs[:, None], (2, per_dev, G, BLOCK, features))
    randoms = fetched.reshape(per_dev, R, 2, BLOCK, features).transpose(2, 0, 1, 3, 4)
    gathered = jnp.concatenate([window, global_slots, randoms], axis=2)
    slot_keys = gathered[0].reshape(per_dev, slots_total, BLOCK, head_count, HD)
    slot_values = gathered[1].reshape(per_dev, slots_total, BLOCK, head_count, HD)
    block_index = device * per_dev + jnp.arange(per_dev)
    glob_index = jnp.arange(G)
    intersections = jnp.abs(glob_index[None, :] - block_index[:, None]) <= 1
    live_slots = jnp.concatenate(
        [
            (block_index >= 1)[:, None],
            jnp.ones((per_dev, 1), jnp.bool_),
            (block_index <= seq_count * per_dev - 2)[:, None],
            jnp.logical_not(intersections),
            jnp.ones((per_dev, R), jnp.bool_),
        ],
        axis=1,
    )
    query_blocks = queries.reshape(per_dev, BLOCK, head_count, HD)
    dout_blocks = out_grads.reshape(per_dev, BLOCK, head_count, HD)
    scores = (
        jnp.einsum("bxhd,bkyhd->bhxky", query_blocks, slot_keys, preferred_element_type=jnp.float32)
        * score_scale
    )
    scores = jnp.where(live_slots[:, None, None, :, None], scores, big_negative)
    row_max = jnp.max(scores, axis=(3, 4), keepdims=True)
    weights = jnp.exp(scores - row_max)
    row_total = jnp.sum(weights, axis=(3, 4), keepdims=True)
    probabilities = weights / row_total
    prob_low = probabilities.astype(jnp.bfloat16)
    prob_grads = jnp.einsum(
        "bxhd,bkyhd->bhxky", dout_blocks, slot_values, preferred_element_type=jnp.float32
    )
    row_dot = jnp.sum(probabilities * prob_grads, axis=(3, 4), keepdims=True)
    score_grads = (probabilities * (prob_grads - row_dot)).astype(jnp.bfloat16)
    query_grads = (
        jnp.einsum("bhxky,bkyhd->bxhd", score_grads, slot_keys, preferred_element_type=jnp.float32)
        * score_scale
    )
    key_terms = (
        jnp.einsum(
            "bhxky,bxhd->bkyhd", score_grads, query_blocks, preferred_element_type=jnp.float32
        )
        * score_scale
    )
    value_terms = jnp.einsum(
        "bhxky,bxhd->bkyhd", prob_low, dout_blocks, preferred_element_type=jnp.float32
    )
    pair_terms = jnp.stack([key_terms, value_terms]).reshape(
        2, per_dev, slots_total, BLOCK, features
    )
    framed_sum = jnp.pad(pair_terms[:, :, 0], ((0, 0), (0, 2), (0, 0), (0, 0)))
    framed_sum = framed_sum + jnp.pad(pair_terms[:, :, 1], ((0, 0), (1, 1), (0, 0), (0, 0)))
    framed_sum = framed_sum + jnp.pad(pair_terms[:, :, 2], ((0, 0), (2, 0), (0, 0), (0, 0)))
    totals = framed_sum[:, 1 : per_dev + 1]
    global_sum = jnp.sum(pair_terms[:, :, 3 : 3 + G], axis=1)
    rim_terms = jnp.concatenate([framed_sum[:, 0], framed_sum[:, -1]], axis=1)
    widened = extended_2(rim_terms.astype(jnp.bfloat16), (("seq", 1),), BLOCK).astype(
        rim_terms.dtype
    )
    totals = totals.at[:, 0].add(widened[:, :BLOCK])
    totals = totals.at[:, per_dev - 1].add(widened[:, -BLOCK:])
    target = jnp.where(my_usable, my_slot, seq_count * capacity)
    rand_terms = (
        pair_terms[:, :, 3 + G :].reshape(2, rand_count, BLOCK, features).transpose(1, 0, 2, 3)
    )
    outgoing_back = (
        jnp.zeros((seq_count * capacity, 2, BLOCK, features), jnp.float32)
        .at[target]
        .set(rand_terms, mode="drop")
    )
    arrived = lax.all_to_all(
        outgoing_back.astype(jnp.bfloat16), "seq", split_axis=0, concat_axis=0, tiled=True
    ).astype(outgoing_back.dtype)
    collected = jnp.einsum(
        "dcb,dcsxf->sbxf",
        chooser,
        arrived.reshape(seq_count, capacity, 2, BLOCK, features),
        precision=lax.Precision.HIGHEST,
    )
    everywhere = lax.psum(global_sum, "seq")
    padded_global = jnp.pad(everywhere, ((0, 0), (0, per_dev - G), (0, 0), (0, 0))) * (
        device == 0
    ).astype(jnp.float32)
    totals = totals + collected + padded_global
    grad_rows = query_grads.reshape(tokens, features).astype(jnp.bfloat16)
    key_rows = totals[0].reshape(tokens, features).astype(jnp.bfloat16)
    value_rows = totals[1].reshape(tokens, features).astype(jnp.bfloat16)
    return (
        lax.all_to_all(grad_rows, "head", split_axis=0, concat_axis=1, tiled=True),
        lax.all_to_all(key_rows, "head", split_axis=0, concat_axis=1, tiled=True),
        lax.all_to_all(value_rows, "head", split_axis=0, concat_axis=1, tiled=True),
    )


LOG2E = 1.4426950408889634


def attend_units(units, block_count, rand_of, q_of, do_of, kf, vf, dkf, dvf, put_dq):
    slots_total = 3 + G + R
    f32, bf16 = jnp.float32, jnp.bfloat16
    lanes = sum(rows for _, rows, _ in units)
    lane = lax.broadcasted_iota(jnp.int32, (1, lanes), 1)
    slot_ids, biases = [], []
    for _, _, j in units:
        slot_ids.append(
            [jnp.maximum(j - 1, 0), j, jnp.minimum(j + 1, block_count - 1)]
            + list(range(G))
            + [rand_of(j, r) for r in range(R)]
        )
        live = {0: j >= 1, 2: j <= block_count - 2}
        for i in range(G):
            live[3 + i] = jnp.abs(i - j) > 1
        biases.append({s: jnp.where(ok, 0.0, big_negative).astype(f32) for s, ok in live.items()})

    def slot_rows(ref, b):
        if isinstance(b, int):
            return ref[b * BLOCK : (b + 1) * BLOCK, :]
        return ref[pl.ds(pl.multiple_of(b * BLOCK, BLOCK), BLOCK), :]

    def side_by_side(ref):
        return jnp.concatenate(
            [jnp.concatenate([slot_rows(ref, b) for b in ids], axis=0) for ids in slot_ids], axis=1
        )

    def diagonal(get):
        strips = []
        for at, (first, rows, _) in enumerate(units):
            blank = jnp.zeros((rows, HD), bf16)
            strips.append(
                jnp.concatenate(
                    [get(first, rows) if i == at else blank for i in range(len(units))], axis=1
                )
            )
        return jnp.concatenate(strips, axis=0)

    k_all, v_all = side_by_side(kf), side_by_side(vf)
    q_diag, do_diag = diagonal(q_of), diagonal(do_of)
    across = (((1,), (1,)), ((), ()))
    raw = lax.dot_general(k_all, q_diag, across, preferred_element_type=f32)
    factor = HD ** (-0.5) * LOG2E
    parts = []
    for s in range(slots_total):
        part = raw[s * BLOCK : (s + 1) * BLOCK] * factor
        if s in biases[0]:
            bias = jnp.full((1, lanes), 0.0, f32) + biases[0][s]
            start = 0
            for at in range(1, len(units)):
                start += units[at - 1][1]
                bias = jnp.where(lane >= start, biases[at][s], bias)
            part = part + bias
        parts.append(part)
    scores = jnp.concatenate(parts, axis=0)
    weights = jnp.exp2(scores - jnp.max(scores, axis=0, keepdims=True))
    probs = weights * (1.0 / jnp.sum(weights, axis=0, keepdims=True))
    prob_grads = lax.dot_general(v_all, do_diag, across, preferred_element_type=f32)
    row_dot = jnp.sum(probs * prob_grads, axis=0, keepdims=True)
    score_grads = (probs * (prob_grads - row_dot)).astype(bf16)
    dv = jnp.dot(probs.astype(bf16), do_diag, preferred_element_type=f32)
    dk = jnp.dot(score_grads, q_diag, preferred_element_type=f32)
    dq = lax.dot_general(
        score_grads, k_all, (((0,), (0,)), ((), ())), preferred_element_type=f32
    ) * (HD ** (-0.5))
    for at, ids in enumerate(slot_ids):
        cols = slice(at * HD, (at + 1) * HD)
        for s, b in enumerate(ids):
            rows = slice(s * BLOCK, (s + 1) * BLOCK)
            if isinstance(b, int):
                where = pl.ds(b * BLOCK, BLOCK)
            else:
                where = pl.ds(pl.multiple_of(b * BLOCK, BLOCK), BLOCK)
            dkf[where, :] += dk[rows, cols]
            dvf[where, :] += dv[rows, cols]
    start = 0
    for at, (first, rows, _) in enumerate(units):
        put_dq(first, rows, dq[start : start + rows, at * HD : (at + 1) * HD].astype(bf16))
        start += rows


def attend_kernel(chunks, core_ref, rand_ref, qd_ref, own_ref, sib_ref, dq_ref, down_ref, dsib_ref,
                  kf, vf, dkf, dvf):
    span = qd_ref.shape[2]
    half = BLOCK // 2
    per_pair = 2 * span // BLOCK
    block_count = chunks * per_pair
    core = core_ref[0]

    def rows_at(g, which):
        return pl.ds(pl.multiple_of(g * 2 * span + which * span, half), span)

    def lay(g, carry):
        mine, other = rows_at(g, core), rows_at(g, 1 - core)
        kf[mine, :] = own_ref[g, 0]
        vf[mine, :] = own_ref[g, 1]
        kf[other, :] = sib_ref[g, 0]
        vf[other, :] = sib_ref[g, 1]
        zeros = jnp.zeros((span, HD), jnp.float32)
        for ref in (dkf, dvf):
            ref[mine, :] = zeros
            ref[other, :] = zeros
        return carry

    lax.fori_loop(0, chunks, lay, 0)

    def run(units):
        attend_units(
            [(first, rows, j) for first, rows, j in units],
            block_count,
            lambda j, r: rand_ref[j * R + r],
            lambda at, rows: qd_ref[at[0], 0, pl.ds(pl.multiple_of(at[1], half), rows), :],
            lambda at, rows: qd_ref[at[0], 1, pl.ds(pl.multiple_of(at[1], half), rows), :],
            kf, vf, dkf, dvf,
            put,
        )

    def put(at, rows, values):
        dq_ref[at[0], pl.ds(pl.multiple_of(at[1], half), rows), :] = values

    def whole_blocks(g, carry):
        run(
            [
                ((g, core * half + i * BLOCK), BLOCK, g * per_pair + core * 3 + i)
                for i in range(2)
            ]
        )
        return carry

    lax.fori_loop(0, chunks, whole_blocks, 0)

    def half_blocks(t, carry):
        run(
            [
                ((t * 4 + i, (1 - core) * 2 * BLOCK), half, (t * 4 + i) * per_pair + 2)
                for i in range(4)
            ]
        )
        return carry

    lax.fori_loop(0, chunks // 4, half_blocks, 0)

    def hand_over(g, carry):
        mine, other = rows_at(g, core), rows_at(g, 1 - core)
        scale = HD ** (-0.5)
        down_ref[g, 0] = dkf[mine, :] * scale
        down_ref[g, 1] = dvf[mine, :]
        dsib_ref[g, 0] = (dkf[other, :] * scale).astype(jnp.bfloat16)
        dsib_ref[g, 1] = dvf[other, :].astype(jnp.bfloat16)
        return carry

    lax.fori_loop(0, chunks, hand_over, 0)


def on_chip_pair(seq_count, head_devices, query, key, value, grad_out, rand_blocks):
    both = ("seq", "head")
    count = seq_count * head_devices
    chunks = count // 2
    groups = [[i for i in range(count) if i % 2 == core] for core in range(2)]
    swap = [(i, i ^ 1) for i in range(head_devices)]
    span = query.shape[0]
    core = lax.rem(lax.axis_index("head"), 2)

    def spread(*arrays):
        cut = jnp.stack([a.reshape(span, chunks, HD).transpose(1, 0, 2) for a in arrays], axis=1)
        return lax.all_to_all(
            cut, both, split_axis=0, concat_axis=0, axis_index_groups=groups, tiled=True
        )

    own = spread(key, value)
    rows = spread(query, grad_out)
    sib = lax.ppermute(own, "head", swap)
    vmem = pl.BlockSpec(memory_space=pltpu.VMEM)
    smem = pl.BlockSpec(memory_space=pltpu.SMEM)
    total = chunks * 2 * span
    dq, down, dsib = pl.pallas_call(
        functools.partial(attend_kernel, chunks),
        out_shape=(
            jax.ShapeDtypeStruct((chunks, span, HD), jnp.bfloat16),
            jax.ShapeDtypeStruct((chunks, 2, span, HD), jnp.float32),
            jax.ShapeDtypeStruct((chunks, 2, span, HD), jnp.bfloat16),
        ),
        in_specs=[smem, smem, vmem, vmem, vmem],
        out_specs=(vmem, vmem, vmem),
        scratch_shapes=[
            pltpu.VMEM((total, HD), jnp.bfloat16),
            pltpu.VMEM((total, HD), jnp.bfloat16),
            pltpu.VMEM((total, HD), jnp.float32),
            pltpu.VMEM((total, HD), jnp.float32),
        ],
        compiler_params=pltpu.CompilerParams(vmem_limit_bytes=40 * 2**20),
    )(core.reshape(1), rand_blocks.reshape(-1), rows, own, sib)
    part = lax.ppermute(dsib, "head", swap)
    summed = (down + part.astype(jnp.float32)).astype(jnp.bfloat16)

    def collect(cut):
        return lax.all_to_all(
            cut, both, split_axis=0, concat_axis=0, axis_index_groups=groups, tiled=True
        )

    def flat(cut):
        return cut.transpose(1, 0, 2).reshape(span, chunks * HD)

    dq = flat(collect(dq))
    both_grads = collect(summed)
    return dq, flat(both_grads[:, 0]), flat(both_grads[:, 1])


def solution(mesh):
    rows = P(("seq", "head"), None)
    seq_count, head_devices = mesh.shape["seq"], mesh.shape["head"]

    def run(query, key, value, grad_out, rand_blocks):
        count = seq_count * head_devices
        heads = query.shape[1] // HD
        span = query.shape[0] // count
        body = on_device
        if head_devices % 2 == 0 and count == 2 * heads and heads % 4 == 0 and 2 * span == 5 * BLOCK:
            body = functools.partial(on_chip_pair, seq_count, head_devices)
        return jax.shard_map(
            body,
            mesh=mesh,
            in_specs=(rows, rows, rows, rows, P()),
            out_specs=(rows, rows, rows),
            check_vma=False,
        )(query, key, value, grad_out, rand_blocks)

    return run
```

```python
import functools

import jax
import jax.numpy as jnp
from jax import lax
from jax.experimental import pallas as pl
from jax.experimental.pallas import tpu as pltpu
from jax.sharding import PartitionSpec as P

HD = 128
BLOCK = 64
G = 2
R = 3


big_negative = -1e30


def broadcast(block, axis, source):
    block = jnp.where(lax.axis_index(axis) == source, block, jnp.zeros_like(block))
    return lax.psum(block, axis)


def extended_2(shard, sides, width):
    for axis, dim in sides:
        peers, length = (lax.axis_size(axis), shard.shape[dim])
        up = [(i, (i + 1) % peers) for i in range(peers - 1)]
        down = [(j, i) for i, j in up]
        last = lax.slice_in_dim(shard, length - width, length, axis=dim)
        leading = lax.slice_in_dim(shard, 0, width, axis=dim)
        before = lax.ppermute(last, axis, up)
        after = lax.ppermute(leading, axis, down)
        shard = jnp.concatenate([before, shard, after], axis=dim)
    return shard


def request_plan(requested, device, per_dev):
    wanted_row = requested[device]
    owners = wanted_row // per_dev
    within = wanted_row % per_dev
    usable = jnp.ones(wanted_row.shape, jnp.bool_)
    positions = jnp.arange(owners.shape[0])
    earlier = (owners[:, None] == owners[None, :]) & (positions[None, :] < positions[:, None])
    slot_rank = jnp.sum(earlier.astype(jnp.int32), axis=1)
    return (owners, within, slot_rank, usable)


def on_device(query, key, value, grad_out, rand_blocks):
    queries, keys, values, out_grads = (
        lax.all_to_all(query, "head", split_axis=1, concat_axis=0, tiled=True),
        lax.all_to_all(key, "head", split_axis=1, concat_axis=0, tiled=True),
        lax.all_to_all(value, "head", split_axis=1, concat_axis=0, tiled=True),
        lax.all_to_all(grad_out, "head", split_axis=1, concat_axis=0, tiled=True),
    )
    tokens, features = queries.shape
    head_count = features // HD
    per_dev = tokens // BLOCK
    seq_count = lax.axis_size("seq")
    device = lax.axis_index("seq")
    capacity = (per_dev * R + seq_count - 3) // (seq_count - 2)
    rand_count = per_dev * R
    slots_total = 3 + G + R
    score_scale = HD ** (-0.5)
    requested = rand_blocks.reshape(seq_count, rand_count)
    owners_all, within_all, rank_all, usable_all = jax.vmap(
        lambda sender: request_plan(requested, sender, per_dev)
    )(jnp.arange(seq_count, dtype=jnp.int32))
    to_me = usable_all & (owners_all == device)
    slot_ids = jnp.arange(capacity)
    block_ids = jnp.arange(per_dev)
    matches = (
        to_me[:, :, None, None]
        & (rank_all[:, :, None, None] == slot_ids[None, None, :, None])
        & (within_all[:, :, None, None] == block_ids[None, None, None, :])
    )
    chooser = jnp.sum(matches.astype(jnp.float32), axis=1)
    my_owners, my_within, my_rank, my_usable = request_plan(requested, device, per_dev)
    my_slot = jnp.clip(my_owners, 0, seq_count - 1) * capacity + my_rank
    own_pairs = jnp.stack([keys, values]).reshape(2, per_dev, BLOCK, features)
    served = None
    served = jnp.einsum(
        "dcb,sbxf->dcsxf",
        chooser.astype(jnp.bfloat16),
        own_pairs,
        preferred_element_type=jnp.float32,
    ).astype(jnp.bfloat16)
    outgoing = served.reshape(seq_count * capacity, 2, BLOCK, features)
    incoming = lax.all_to_all(outgoing, "seq", split_axis=0, concat_axis=0, tiled=True)
    wanted = (my_slot[:, None] == jnp.arange(seq_count * capacity)[None, :]).astype(jnp.bfloat16)
    fetched = jnp.einsum(
        "ro,osxf->rsxf", wanted, incoming, preferred_element_type=jnp.float32
    ).astype(jnp.bfloat16)
    leading = jnp.stack([keys[: G * BLOCK], values[: G * BLOCK]])
    global_pairs = broadcast(leading, "seq", 0).reshape(2, G, BLOCK, features)
    extended = extended_2(jnp.stack([keys, values]), (("seq", 1),), BLOCK)
    left_pair = extended[:, :BLOCK]
    right_pair = extended[:, -BLOCK:]
    framed = jnp.concatenate([left_pair[:, None], own_pairs, right_pair[:, None]], axis=1)
    window = jnp.stack(
        [framed[:, 0:per_dev], framed[:, 1 : per_dev + 1], framed[:, 2 : per_dev + 2]], axis=2
    )
    global_slots = jnp.broadcast_to(global_pairs[:, None], (2, per_dev, G, BLOCK, features))
    randoms = fetched.reshape(per_dev, R, 2, BLOCK, features).transpose(2, 0, 1, 3, 4)
    gathered = jnp.concatenate([window, global_slots, randoms], axis=2)
    slot_keys = gathered[0].reshape(per_dev, slots_total, BLOCK, head_count, HD)
    slot_values = gathered[1].reshape(per_dev, slots_total, BLOCK, head_count, HD)
    block_index = device * per_dev + jnp.arange(per_dev)
    glob_index = jnp.arange(G)
    intersections = jnp.abs(glob_index[None, :] - block_index[:, None]) <= 1
    live_slots = jnp.concatenate(
        [
            (block_index >= 1)[:, None],
            jnp.ones((per_dev, 1), jnp.bool_),
            (block_index <= seq_count * per_dev - 2)[:, None],
            jnp.logical_not(intersections),
            jnp.ones((per_dev, R), jnp.bool_),
        ],
        axis=1,
    )
    query_blocks = queries.reshape(per_dev, BLOCK, head_count, HD)
    dout_blocks = out_grads.reshape(per_dev, BLOCK, head_count, HD)
    scores = (
        jnp.einsum("bxhd,bkyhd->bhxky", query_blocks, slot_keys, preferred_element_type=jnp.float32)
        * score_scale
    )
    scores = jnp.where(live_slots[:, None, None, :, None], scores, big_negative)
    row_max = jnp.max(scores, axis=(3, 4), keepdims=True)
    weights = jnp.exp(scores - row_max)
    row_total = jnp.sum(weights, axis=(3, 4), keepdims=True)
    probabilities = weights / row_total
    prob_low = probabilities.astype(jnp.bfloat16)
    prob_grads = jnp.einsum(
        "bxhd,bkyhd->bhxky", dout_blocks, slot_values, preferred_element_type=jnp.float32
    )
    row_dot = jnp.sum(probabilities * prob_grads, axis=(3, 4), keepdims=True)
    score_grads = (probabilities * (prob_grads - row_dot)).astype(jnp.bfloat16)
    query_grads = (
        jnp.einsum("bhxky,bkyhd->bxhd", score_grads, slot_keys, preferred_element_type=jnp.float32)
        * score_scale
    )
    key_terms = (
        jnp.einsum(
            "bhxky,bxhd->bkyhd", score_grads, query_blocks, preferred_element_type=jnp.float32
        )
        * score_scale
    )
    value_terms = jnp.einsum(
        "bhxky,bxhd->bkyhd", prob_low, dout_blocks, preferred_element_type=jnp.float32
    )
    pair_terms = jnp.stack([key_terms, value_terms]).reshape(
        2, per_dev, slots_total, BLOCK, features
    )
    framed_sum = jnp.pad(pair_terms[:, :, 0], ((0, 0), (0, 2), (0, 0), (0, 0)))
    framed_sum = framed_sum + jnp.pad(pair_terms[:, :, 1], ((0, 0), (1, 1), (0, 0), (0, 0)))
    framed_sum = framed_sum + jnp.pad(pair_terms[:, :, 2], ((0, 0), (2, 0), (0, 0), (0, 0)))
    totals = framed_sum[:, 1 : per_dev + 1]
    global_sum = jnp.sum(pair_terms[:, :, 3 : 3 + G], axis=1)
    rim_terms = jnp.concatenate([framed_sum[:, 0], framed_sum[:, -1]], axis=1)
    widened = extended_2(rim_terms.astype(jnp.bfloat16), (("seq", 1),), BLOCK).astype(
        rim_terms.dtype
    )
    totals = totals.at[:, 0].add(widened[:, :BLOCK])
    totals = totals.at[:, per_dev - 1].add(widened[:, -BLOCK:])
    target = jnp.where(my_usable, my_slot, seq_count * capacity)
    rand_terms = (
        pair_terms[:, :, 3 + G :].reshape(2, rand_count, BLOCK, features).transpose(1, 0, 2, 3)
    )
    outgoing_back = (
        jnp.zeros((seq_count * capacity, 2, BLOCK, features), jnp.float32)
        .at[target]
        .set(rand_terms, mode="drop")
    )
    arrived = lax.all_to_all(
        outgoing_back.astype(jnp.bfloat16), "seq", split_axis=0, concat_axis=0, tiled=True
    ).astype(outgoing_back.dtype)
    collected = jnp.einsum(
        "dcb,dcsxf->sbxf",
        chooser,
        arrived.reshape(seq_count, capacity, 2, BLOCK, features),
        precision=lax.Precision.HIGHEST,
    )
    everywhere = lax.psum(global_sum, "seq")
    padded_global = jnp.pad(everywhere, ((0, 0), (0, per_dev - G), (0, 0), (0, 0))) * (
        device == 0
    ).astype(jnp.float32)
    totals = totals + collected + padded_global
    grad_rows = query_grads.reshape(tokens, features).astype(jnp.bfloat16)
    key_rows = totals[0].reshape(tokens, features).astype(jnp.bfloat16)
    value_rows = totals[1].reshape(tokens, features).astype(jnp.bfloat16)
    return (
        lax.all_to_all(grad_rows, "head", split_axis=0, concat_axis=1, tiled=True),
        lax.all_to_all(key_rows, "head", split_axis=0, concat_axis=1, tiled=True),
        lax.all_to_all(value_rows, "head", split_axis=0, concat_axis=1, tiled=True),
    )


LOG2E = 1.4426950408889634


def attend_units(units, block_count, rand_of, q_of, do_of, kf, vf, dkf, dvf, put_dq):
    slots_total = 3 + G + R
    f32, bf16 = jnp.float32, jnp.bfloat16
    lanes = sum(rows for _, rows, _ in units)
    lane = lax.broadcasted_iota(jnp.int32, (1, lanes), 1)
    slot_ids, biases = [], []
    for _, _, j in units:
        slot_ids.append(
            [jnp.maximum(j - 1, 0), j, jnp.minimum(j + 1, block_count - 1)]
            + list(range(G))
            + [rand_of(j, r) for r in range(R)]
        )
        live = {0: j >= 1, 2: j <= block_count - 2}
        for i in range(G):
            live[3 + i] = jnp.abs(i - j) > 1
        biases.append({s: jnp.where(ok, 0.0, big_negative).astype(f32) for s, ok in live.items()})

    def slot_rows(ref, b):
        if isinstance(b, int):
            return ref[b * BLOCK : (b + 1) * BLOCK, :]
        return ref[pl.ds(pl.multiple_of(b * BLOCK, BLOCK), BLOCK), :]

    def side_by_side(ref):
        return jnp.concatenate(
            [jnp.concatenate([slot_rows(ref, b) for b in ids], axis=0) for ids in slot_ids], axis=1
        )

    def diagonal(get):
        strips = []
        for at, (first, rows, _) in enumerate(units):
            blank = jnp.zeros((rows, HD), bf16)
            strips.append(
                jnp.concatenate(
                    [get(first, rows) if i == at else blank for i in range(len(units))], axis=1
                )
            )
        return jnp.concatenate(strips, axis=0)

    k_all, v_all = side_by_side(kf), side_by_side(vf)
    q_diag, do_diag = diagonal(q_of), diagonal(do_of)
    across = (((1,), (1,)), ((), ()))
    raw = lax.dot_general(k_all, q_diag, across, preferred_element_type=f32)
    factor = HD ** (-0.5) * LOG2E
    parts = []
    for s in range(slots_total):
        part = raw[s * BLOCK : (s + 1) * BLOCK] * factor
        if s in biases[0]:
            bias = jnp.full((1, lanes), 0.0, f32) + biases[0][s]
            start = 0
            for at in range(1, len(units)):
                start += units[at - 1][1]
                bias = jnp.where(lane >= start, biases[at][s], bias)
            part = part + bias
        parts.append(part)
    scores = jnp.concatenate(parts, axis=0)
    weights = jnp.exp2(scores - jnp.max(scores, axis=0, keepdims=True))
    probs = weights * (1.0 / jnp.sum(weights, axis=0, keepdims=True))
    prob_grads = lax.dot_general(v_all, do_diag, across, preferred_element_type=f32)
    row_dot = jnp.sum(probs * prob_grads, axis=0, keepdims=True)
    score_grads = (probs * (prob_grads - row_dot)).astype(bf16)
    dv = jnp.dot(probs.astype(bf16), do_diag, preferred_element_type=f32)
    dk = jnp.dot(score_grads, q_diag, preferred_element_type=f32)
    dq = lax.dot_general(
        score_grads, k_all, (((0,), (0,)), ((), ())), preferred_element_type=f32
    ) * (HD ** (-0.5))
    for at, ids in enumerate(slot_ids):
        cols = slice(at * HD, (at + 1) * HD)
        for s, b in enumerate(ids):
            rows = slice(s * BLOCK, (s + 1) * BLOCK)
            if isinstance(b, int):
                where = pl.ds(b * BLOCK, BLOCK)
            else:
                where = pl.ds(pl.multiple_of(b * BLOCK, BLOCK), BLOCK)
            dkf[where, :] += dk[rows, cols]
            dvf[where, :] += dv[rows, cols]
    start = 0
    for at, (first, rows, _) in enumerate(units):
        put_dq(first, rows, dq[start : start + rows, at * HD : (at + 1) * HD].astype(bf16))
        start += rows


def rows_at(g, which, span):
    return pl.ds(pl.multiple_of(g * 2 * span + which * span, BLOCK // 2), span)


def whole_kernel(chunks, span, core_ref, rand_ref, in_ref, sib_ref, dq_ref, kf, vf, dkf, dvf):
    per_pair = 2 * span // BLOCK
    core = core_ref[0]
    many = 2 * BLOCK

    def lay(g, carry):
        mine, other = rows_at(g, core, span), rows_at(g, 1 - core, span)
        kf[mine, :] = in_ref[g, :span]
        vf[mine, :] = in_ref[g, span : 2 * span]
        kf[other, :] = sib_ref[g, :span]
        vf[other, :] = sib_ref[g, span:]
        zeros = jnp.zeros((span, HD), jnp.float32)
        for ref in (dkf, dvf):
            ref[mine, :] = zeros
            ref[other, :] = zeros
        return carry

    lax.fori_loop(0, chunks, lay, 0)

    def put(at, rows, values):
        dq_ref[at[0], at[1] : at[1] + rows] = values

    def whole_blocks(g, carry):
        q_at, do_at = 2 * span, 2 * span + many
        attend_units(
            [((g, i * BLOCK), BLOCK, g * per_pair + core * 3 + i) for i in range(2)],
            chunks * per_pair,
            lambda j, r: rand_ref[j * R + r],
            lambda at, rows: in_ref[at[0], q_at + at[1] : q_at + at[1] + rows],
            lambda at, rows: in_ref[at[0], do_at + at[1] : do_at + at[1] + rows],
            kf, vf, dkf, dvf, put,
        )
        return carry

    lax.fori_loop(0, chunks, whole_blocks, 0)


def half_kernel(chunks, span, core_ref, rand_ref, in_ref, kf, vf, dk_ref, dv_ref,
                dq_ref, down_ref, dsib_ref, dkf, dvf):
    per_pair = 2 * span // BLOCK
    core = core_ref[0]
    half = BLOCK // 2

    def lay(g, carry):
        for which in range(2):
            rows = rows_at(g, which, span)
            dkf[rows, :] = dk_ref[rows, :]
            dvf[rows, :] = dv_ref[rows, :]
        return carry

    lax.fori_loop(0, chunks, lay, 0)

    def put(at, rows, values):
        dq_ref[at] = values

    def half_blocks(t, carry):
        attend_units(
            [(t * 4 + i, half, (t * 4 + i) * per_pair + 2) for i in range(4)],
            chunks * per_pair,
            lambda j, r: rand_ref[j * R + r],
            lambda at, rows: in_ref[at, :rows],
            lambda at, rows: in_ref[at, rows:],
            kf, vf, dkf, dvf, put,
        )
        return carry

    lax.fori_loop(0, chunks // 4, half_blocks, 0)

    def hand_over(g, carry):
        mine, other = rows_at(g, core, span), rows_at(g, 1 - core, span)
        scale = HD ** (-0.5)
        down_ref[g, :span] = dkf[mine, :] * scale
        down_ref[g, span:] = dvf[mine, :]
        dsib_ref[g, :span] = (dkf[other, :] * scale).astype(jnp.bfloat16)
        dsib_ref[g, span:] = dvf[other, :].astype(jnp.bfloat16)
        return carry

    lax.fori_loop(0, chunks, hand_over, 0)


def on_chip_pair(seq_count, head_devices, query, key, value, grad_out, rand_blocks):
    both = ("seq", "head")
    count = seq_count * head_devices
    chunks = count // 2
    groups = [[i for i in range(count) if i % 2 == core] for core in range(2)]
    swap = [(i, i ^ 1) for i in range(head_devices)]
    span = query.shape[0]
    half, many = BLOCK // 2, 2 * BLOCK
    core = lax.rem(lax.axis_index("head"), 2)

    def exchange(cut):
        return lax.all_to_all(
            cut, both, split_axis=0, concat_axis=0, axis_index_groups=groups, tiled=True
        )

    def spread(*arrays):
        rows = jnp.concatenate(arrays, axis=0)
        return exchange(rows.reshape(rows.shape[0], chunks, HD).transpose(1, 0, 2))

    def wholes(a):
        return lax.dynamic_slice_in_dim(a, core * half, many, axis=0)

    def halves(a):
        return lax.dynamic_slice_in_dim(a, (1 - core) * many, half, axis=0)

    first = spread(key, value, wholes(query), wholes(grad_out))
    second = spread(halves(query), halves(grad_out))
    sib = lax.ppermute(first[:, : 2 * span], "head", swap)
    vmem = pl.BlockSpec(memory_space=pltpu.VMEM)
    smem = pl.BlockSpec(memory_space=pltpu.SMEM)
    total = chunks * 2 * span
    held = jax.ShapeDtypeStruct((total, HD), jnp.bfloat16)
    sums = jax.ShapeDtypeStruct((total, HD), jnp.float32)
    place, table = core.reshape(1), rand_blocks.reshape(-1)
    params = pltpu.CompilerParams(vmem_limit_bytes=40 * 2**20)
    dq_whole, kf, vf, dkf, dvf = pl.pallas_call(
        functools.partial(whole_kernel, chunks, span),
        out_shape=(jax.ShapeDtypeStruct((chunks, many, HD), jnp.bfloat16), held, held, sums, sums),
        in_specs=[smem, smem, vmem, vmem],
        out_specs=(vmem,) * 5,
        compiler_params=params,
        cost_estimate=pl.CostEstimate(flops=14 * 10**9, bytes_accessed=12 * 10**6, transcendentals=0),
    )(place, table, first, sib)
    got_whole = exchange(dq_whole)
    dq_half, down, dsib = pl.pallas_call(
        functools.partial(half_kernel, chunks, span),
        out_shape=(
            jax.ShapeDtypeStruct((chunks, half, HD), jnp.bfloat16),
            jax.ShapeDtypeStruct((chunks, 2 * span, HD), jnp.float32),
            jax.ShapeDtypeStruct((chunks, 2 * span, HD), jnp.bfloat16),
        ),
        in_specs=[smem, smem] + [vmem] * 5,
        out_specs=(vmem,) * 3,
        scratch_shapes=[pltpu.VMEM((total, HD), jnp.float32)] * 2,
        compiler_params=params,
        cost_estimate=pl.CostEstimate(flops=6 * 10**9, bytes_accessed=12 * 10**6, transcendentals=0),
    )(place, table, second, kf, vf, dkf, dvf)
    dsib, got_whole = lax.optimization_barrier((dsib, got_whole))
    part = lax.ppermute(dsib, "head", swap)
    summed = (down + part.astype(jnp.float32)).astype(jnp.bfloat16)
    last = exchange(jnp.concatenate([summed, dq_half], axis=1))

    def flat(cut):
        return cut.transpose(1, 0, 2).reshape(cut.shape[1], chunks * HD)

    got_half = last[:, 2 * span :]
    dq = jnp.where(
        core == 0,
        jnp.concatenate([got_whole, got_half], axis=1),
        jnp.concatenate([got_half, got_whole], axis=1),
    )
    return flat(dq), flat(last[:, :span]), flat(last[:, span : 2 * span])


def solution(mesh):
    rows = P(("seq", "head"), None)
    seq_count, head_devices = mesh.shape["seq"], mesh.shape["head"]

    def run(query, key, value, grad_out, rand_blocks):
        count = seq_count * head_devices
        heads = query.shape[1] // HD
        span = query.shape[0] // count
        body = on_device
        if head_devices % 2 == 0 and count == 2 * heads and heads % 4 == 0 and 2 * span == 5 * BLOCK:
            body = functools.partial(on_chip_pair, seq_count, head_devices)
        return jax.shard_map(
            body,
            mesh=mesh,
            in_specs=(rows, rows, rows, rows, P()),
            out_specs=(rows, rows, rows),
            check_vma=False,
        )(query, key, value, grad_out, rand_blocks)

    return run
```

```python
import functools

import jax
import jax.numpy as jnp
from jax import lax
from jax.experimental import pallas as pl
from jax.experimental.pallas import tpu as pltpu
from jax.sharding import PartitionSpec as P

HD = 128
BLOCK = 64
G = 2
R = 3


big_negative = -1e30


def broadcast(block, axis, source):
    block = jnp.where(lax.axis_index(axis) == source, block, jnp.zeros_like(block))
    return lax.psum(block, axis)


def extended_2(shard, sides, width):
    for axis, dim in sides:
        peers, length = (lax.axis_size(axis), shard.shape[dim])
        up = [(i, (i + 1) % peers) for i in range(peers - 1)]
        down = [(j, i) for i, j in up]
        last = lax.slice_in_dim(shard, length - width, length, axis=dim)
        leading = lax.slice_in_dim(shard, 0, width, axis=dim)
        before = lax.ppermute(last, axis, up)
        after = lax.ppermute(leading, axis, down)
        shard = jnp.concatenate([before, shard, after], axis=dim)
    return shard


def request_plan(requested, device, per_dev):
    wanted_row = requested[device]
    owners = wanted_row // per_dev
    within = wanted_row % per_dev
    usable = jnp.ones(wanted_row.shape, jnp.bool_)
    positions = jnp.arange(owners.shape[0])
    earlier = (owners[:, None] == owners[None, :]) & (positions[None, :] < positions[:, None])
    slot_rank = jnp.sum(earlier.astype(jnp.int32), axis=1)
    return (owners, within, slot_rank, usable)


def on_device(query, key, value, grad_out, rand_blocks):
    queries, keys, values, out_grads = (
        lax.all_to_all(query, "head", split_axis=1, concat_axis=0, tiled=True),
        lax.all_to_all(key, "head", split_axis=1, concat_axis=0, tiled=True),
        lax.all_to_all(value, "head", split_axis=1, concat_axis=0, tiled=True),
        lax.all_to_all(grad_out, "head", split_axis=1, concat_axis=0, tiled=True),
    )
    tokens, features = queries.shape
    head_count = features // HD
    per_dev = tokens // BLOCK
    seq_count = lax.axis_size("seq")
    device = lax.axis_index("seq")
    capacity = (per_dev * R + seq_count - 3) // (seq_count - 2)
    rand_count = per_dev * R
    slots_total = 3 + G + R
    score_scale = HD ** (-0.5)
    requested = rand_blocks.reshape(seq_count, rand_count)
    owners_all, within_all, rank_all, usable_all = jax.vmap(
        lambda sender: request_plan(requested, sender, per_dev)
    )(jnp.arange(seq_count, dtype=jnp.int32))
    to_me = usable_all & (owners_all == device)
    slot_ids = jnp.arange(capacity)
    block_ids = jnp.arange(per_dev)
    matches = (
        to_me[:, :, None, None]
        & (rank_all[:, :, None, None] == slot_ids[None, None, :, None])
        & (within_all[:, :, None, None] == block_ids[None, None, None, :])
    )
    chooser = jnp.sum(matches.astype(jnp.float32), axis=1)
    my_owners, my_within, my_rank, my_usable = request_plan(requested, device, per_dev)
    my_slot = jnp.clip(my_owners, 0, seq_count - 1) * capacity + my_rank
    own_pairs = jnp.stack([keys, values]).reshape(2, per_dev, BLOCK, features)
    served = None
    served = jnp.einsum(
        "dcb,sbxf->dcsxf",
        chooser.astype(jnp.bfloat16),
        own_pairs,
        preferred_element_type=jnp.float32,
    ).astype(jnp.bfloat16)
    outgoing = served.reshape(seq_count * capacity, 2, BLOCK, features)
    incoming = lax.all_to_all(outgoing, "seq", split_axis=0, concat_axis=0, tiled=True)
    wanted = (my_slot[:, None] == jnp.arange(seq_count * capacity)[None, :]).astype(jnp.bfloat16)
    fetched = jnp.einsum(
        "ro,osxf->rsxf", wanted, incoming, preferred_element_type=jnp.float32
    ).astype(jnp.bfloat16)
    leading = jnp.stack([keys[: G * BLOCK], values[: G * BLOCK]])
    global_pairs = broadcast(leading, "seq", 0).reshape(2, G, BLOCK, features)
    extended = extended_2(jnp.stack([keys, values]), (("seq", 1),), BLOCK)
    left_pair = extended[:, :BLOCK]
    right_pair = extended[:, -BLOCK:]
    framed = jnp.concatenate([left_pair[:, None], own_pairs, right_pair[:, None]], axis=1)
    window = jnp.stack(
        [framed[:, 0:per_dev], framed[:, 1 : per_dev + 1], framed[:, 2 : per_dev + 2]], axis=2
    )
    global_slots = jnp.broadcast_to(global_pairs[:, None], (2, per_dev, G, BLOCK, features))
    randoms = fetched.reshape(per_dev, R, 2, BLOCK, features).transpose(2, 0, 1, 3, 4)
    gathered = jnp.concatenate([window, global_slots, randoms], axis=2)
    slot_keys = gathered[0].reshape(per_dev, slots_total, BLOCK, head_count, HD)
    slot_values = gathered[1].reshape(per_dev, slots_total, BLOCK, head_count, HD)
    block_index = device * per_dev + jnp.arange(per_dev)
    glob_index = jnp.arange(G)
    intersections = jnp.abs(glob_index[None, :] - block_index[:, None]) <= 1
    live_slots = jnp.concatenate(
        [
            (block_index >= 1)[:, None],
            jnp.ones((per_dev, 1), jnp.bool_),
            (block_index <= seq_count * per_dev - 2)[:, None],
            jnp.logical_not(intersections),
            jnp.ones((per_dev, R), jnp.bool_),
        ],
        axis=1,
    )
    query_blocks = queries.reshape(per_dev, BLOCK, head_count, HD)
    dout_blocks = out_grads.reshape(per_dev, BLOCK, head_count, HD)
    scores = (
        jnp.einsum("bxhd,bkyhd->bhxky", query_blocks, slot_keys, preferred_element_type=jnp.float32)
        * score_scale
    )
    scores = jnp.where(live_slots[:, None, None, :, None], scores, big_negative)
    row_max = jnp.max(scores, axis=(3, 4), keepdims=True)
    weights = jnp.exp(scores - row_max)
    row_total = jnp.sum(weights, axis=(3, 4), keepdims=True)
    probabilities = weights / row_total
    prob_low = probabilities.astype(jnp.bfloat16)
    prob_grads = jnp.einsum(
        "bxhd,bkyhd->bhxky", dout_blocks, slot_values, preferred_element_type=jnp.float32
    )
    row_dot = jnp.sum(probabilities * prob_grads, axis=(3, 4), keepdims=True)
    score_grads = (probabilities * (prob_grads - row_dot)).astype(jnp.bfloat16)
    query_grads = (
        jnp.einsum("bhxky,bkyhd->bxhd", score_grads, slot_keys, preferred_element_type=jnp.float32)
        * score_scale
    )
    key_terms = (
        jnp.einsum(
            "bhxky,bxhd->bkyhd", score_grads, query_blocks, preferred_element_type=jnp.float32
        )
        * score_scale
    )
    value_terms = jnp.einsum(
        "bhxky,bxhd->bkyhd", prob_low, dout_blocks, preferred_element_type=jnp.float32
    )
    pair_terms = jnp.stack([key_terms, value_terms]).reshape(
        2, per_dev, slots_total, BLOCK, features
    )
    framed_sum = jnp.pad(pair_terms[:, :, 0], ((0, 0), (0, 2), (0, 0), (0, 0)))
    framed_sum = framed_sum + jnp.pad(pair_terms[:, :, 1], ((0, 0), (1, 1), (0, 0), (0, 0)))
    framed_sum = framed_sum + jnp.pad(pair_terms[:, :, 2], ((0, 0), (2, 0), (0, 0), (0, 0)))
    totals = framed_sum[:, 1 : per_dev + 1]
    global_sum = jnp.sum(pair_terms[:, :, 3 : 3 + G], axis=1)
    rim_terms = jnp.concatenate([framed_sum[:, 0], framed_sum[:, -1]], axis=1)
    widened = extended_2(rim_terms.astype(jnp.bfloat16), (("seq", 1),), BLOCK).astype(
        rim_terms.dtype
    )
    totals = totals.at[:, 0].add(widened[:, :BLOCK])
    totals = totals.at[:, per_dev - 1].add(widened[:, -BLOCK:])
    target = jnp.where(my_usable, my_slot, seq_count * capacity)
    rand_terms = (
        pair_terms[:, :, 3 + G :].reshape(2, rand_count, BLOCK, features).transpose(1, 0, 2, 3)
    )
    outgoing_back = (
        jnp.zeros((seq_count * capacity, 2, BLOCK, features), jnp.float32)
        .at[target]
        .set(rand_terms, mode="drop")
    )
    arrived = lax.all_to_all(
        outgoing_back.astype(jnp.bfloat16), "seq", split_axis=0, concat_axis=0, tiled=True
    ).astype(outgoing_back.dtype)
    collected = jnp.einsum(
        "dcb,dcsxf->sbxf",
        chooser,
        arrived.reshape(seq_count, capacity, 2, BLOCK, features),
        precision=lax.Precision.HIGHEST,
    )
    everywhere = lax.psum(global_sum, "seq")
    padded_global = jnp.pad(everywhere, ((0, 0), (0, per_dev - G), (0, 0), (0, 0))) * (
        device == 0
    ).astype(jnp.float32)
    totals = totals + collected + padded_global
    grad_rows = query_grads.reshape(tokens, features).astype(jnp.bfloat16)
    key_rows = totals[0].reshape(tokens, features).astype(jnp.bfloat16)
    value_rows = totals[1].reshape(tokens, features).astype(jnp.bfloat16)
    return (
        lax.all_to_all(grad_rows, "head", split_axis=0, concat_axis=1, tiled=True),
        lax.all_to_all(key_rows, "head", split_axis=0, concat_axis=1, tiled=True),
        lax.all_to_all(value_rows, "head", split_axis=0, concat_axis=1, tiled=True),
    )


LOG2E = 1.4426950408889634


def attend_units(units, block_count, rand_of, q_of, do_of, kf, vf, dkf, dvf, put_dq):
    slots_total = 3 + G + R
    f32, bf16 = jnp.float32, jnp.bfloat16
    lanes = sum(rows for _, rows, _ in units)
    lane = lax.broadcasted_iota(jnp.int32, (1, lanes), 1)
    slot_ids, biases = [], []
    for _, _, j in units:
        slot_ids.append(
            [jnp.maximum(j - 1, 0), j, jnp.minimum(j + 1, block_count - 1)]
            + list(range(G))
            + [rand_of(j, r) for r in range(R)]
        )
        live = {0: j >= 1, 2: j <= block_count - 2}
        for i in range(G):
            live[3 + i] = jnp.abs(i - j) > 1
        biases.append({s: jnp.where(ok, 0.0, big_negative).astype(f32) for s, ok in live.items()})

    def slot_rows(ref, b):
        if isinstance(b, int):
            return ref[b * BLOCK : (b + 1) * BLOCK, :]
        return ref[pl.ds(pl.multiple_of(b * BLOCK, BLOCK), BLOCK), :]

    def side_by_side(ref):
        return jnp.concatenate(
            [jnp.concatenate([slot_rows(ref, b) for b in ids], axis=0) for ids in slot_ids], axis=1
        )

    def diagonal(get):
        strips = []
        for at, (first, rows, _) in enumerate(units):
            blank = jnp.zeros((rows, HD), bf16)
            strips.append(
                jnp.concatenate(
                    [get(first, rows) if i == at else blank for i in range(len(units))], axis=1
                )
            )
        return jnp.concatenate(strips, axis=0)

    k_all, v_all = side_by_side(kf), side_by_side(vf)
    q_diag, do_diag = diagonal(q_of), diagonal(do_of)
    across = (((1,), (1,)), ((), ()))
    raw = lax.dot_general(k_all, q_diag, across, preferred_element_type=f32)
    factor = HD ** (-0.5) * LOG2E
    parts = []
    for s in range(slots_total):
        part = raw[s * BLOCK : (s + 1) * BLOCK] * factor
        if s in biases[0]:
            bias = jnp.full((1, lanes), 0.0, f32) + biases[0][s]
            start = 0
            for at in range(1, len(units)):
                start += units[at - 1][1]
                bias = jnp.where(lane >= start, biases[at][s], bias)
            part = part + bias
        parts.append(part)
    scores = jnp.concatenate(parts, axis=0)
    weights = jnp.exp2(scores - jnp.max(scores, axis=0, keepdims=True))
    probs = weights * (1.0 / jnp.sum(weights, axis=0, keepdims=True))
    prob_grads = lax.dot_general(v_all, do_diag, across, preferred_element_type=f32)
    row_dot = jnp.sum(probs * prob_grads, axis=0, keepdims=True)
    score_grads = (probs * (prob_grads - row_dot)).astype(bf16)
    dv = jnp.dot(probs.astype(bf16), do_diag, preferred_element_type=f32)
    dk = jnp.dot(score_grads, q_diag, preferred_element_type=f32)
    dq = lax.dot_general(
        score_grads, k_all, (((0,), (0,)), ((), ())), preferred_element_type=f32
    ) * (HD ** (-0.5))
    for at, ids in enumerate(slot_ids):
        cols = slice(at * HD, (at + 1) * HD)
        for s, b in enumerate(ids):
            rows = slice(s * BLOCK, (s + 1) * BLOCK)
            if isinstance(b, int):
                where = pl.ds(b * BLOCK, BLOCK)
            else:
                where = pl.ds(pl.multiple_of(b * BLOCK, BLOCK), BLOCK)
            dkf[where, :] += dk[rows, cols]
            dvf[where, :] += dv[rows, cols]
    start = 0
    for at, (first, rows, _) in enumerate(units):
        put_dq(first, rows, dq[start : start + rows, at * HD : (at + 1) * HD].astype(bf16))
        start += rows


def rows_at(g, which, span):
    return pl.ds(pl.multiple_of(g * 2 * span + which * span, BLOCK // 2), span)


def whole_kernel(chunks, span, core_ref, rand_ref, in_ref, sib_ref, dq_ref, kf, vf, dkf, dvf):
    per_pair = 2 * span // BLOCK
    core = core_ref[0]
    many = 2 * BLOCK

    def lay(g, carry):
        mine, other = rows_at(g, core, span), rows_at(g, 1 - core, span)
        kf[mine, :] = in_ref[g, :span]
        vf[mine, :] = in_ref[g, span : 2 * span]
        kf[other, :] = sib_ref[g, :span]
        vf[other, :] = sib_ref[g, span:]
        zeros = jnp.zeros((span, HD), jnp.float32)
        for ref in (dkf, dvf):
            ref[mine, :] = zeros
            ref[other, :] = zeros
        return carry

    lax.fori_loop(0, chunks, lay, 0)

    def put(at, rows, values):
        dq_ref[at[0], at[1] : at[1] + rows] = values

    def whole_blocks(g, carry):
        q_at, do_at = 2 * span, 2 * span + many
        attend_units(
            [((g, i * BLOCK), BLOCK, g * per_pair + core * 3 + i) for i in range(2)],
            chunks * per_pair,
            lambda j, r: rand_ref[j * R + r],
            lambda at, rows: in_ref[at[0], q_at + at[1] : q_at + at[1] + rows],
            lambda at, rows: in_ref[at[0], do_at + at[1] : do_at + at[1] + rows],
            kf, vf, dkf, dvf, put,
        )
        return carry

    lax.fori_loop(0, chunks, whole_blocks, 0)


def half_kernel(chunks, span, core_ref, rand_ref, in_ref, kf, vf, dk_ref, dv_ref,
                dq_ref, down_ref, dsib_ref, dkf, dvf):
    per_pair = 2 * span // BLOCK
    core = core_ref[0]
    half = BLOCK // 2

    def lay(g, carry):
        for which in range(2):
            rows = rows_at(g, which, span)
            dkf[rows, :] = dk_ref[rows, :]
            dvf[rows, :] = dv_ref[rows, :]
        return carry

    lax.fori_loop(0, chunks, lay, 0)

    def put(at, rows, values):
        dq_ref[at] = values

    def half_blocks(t, carry):
        attend_units(
            [(t * 4 + i, half, (t * 4 + i) * per_pair + 2) for i in range(4)],
            chunks * per_pair,
            lambda j, r: rand_ref[j * R + r],
            lambda at, rows: in_ref[at, :rows],
            lambda at, rows: in_ref[at, rows:],
            kf, vf, dkf, dvf, put,
        )
        return carry

    lax.fori_loop(0, chunks // 4, half_blocks, 0)

    def hand_over(g, carry):
        mine, other = rows_at(g, core, span), rows_at(g, 1 - core, span)
        scale = HD ** (-0.5)
        down_ref[g, :span] = dkf[mine, :] * scale
        down_ref[g, span:] = dvf[mine, :]
        dsib_ref[g, :span] = (dkf[other, :] * scale).astype(jnp.bfloat16)
        dsib_ref[g, span:] = dvf[other, :].astype(jnp.bfloat16)
        return carry

    lax.fori_loop(0, chunks, hand_over, 0)


def on_chip_pair(seq_count, head_devices, query, key, value, grad_out, rand_blocks):
    both = ("seq", "head")
    count = seq_count * head_devices
    chunks = count // 2
    groups = [[i for i in range(count) if i % 2 == core] for core in range(2)]
    swap = [(i, i ^ 1) for i in range(head_devices)]
    span = query.shape[0]
    half, many = BLOCK // 2, 2 * BLOCK
    core = lax.rem(lax.axis_index("head"), 2)

    def exchange(cut):
        return lax.all_to_all(
            cut, both, split_axis=0, concat_axis=0, axis_index_groups=groups, tiled=True
        )

    def spread(*arrays):
        rows = jnp.concatenate(arrays, axis=0)
        return exchange(rows.reshape(rows.shape[0], chunks, HD).transpose(1, 0, 2))

    def wholes(a):
        return lax.dynamic_slice_in_dim(a, core * half, many, axis=0)

    def halves(a):
        return lax.dynamic_slice_in_dim(a, (1 - core) * many, half, axis=0)

    first = spread(
        key, value, wholes(query), wholes(grad_out), halves(query), halves(grad_out)
    )
    second = first[:, 2 * span + 2 * many :]
    sib = lax.ppermute(first[:, : 2 * span], "head", swap)
    vmem = pl.BlockSpec(memory_space=pltpu.VMEM)
    smem = pl.BlockSpec(memory_space=pltpu.SMEM)
    total = chunks * 2 * span
    held = jax.ShapeDtypeStruct((total, HD), jnp.bfloat16)
    sums = jax.ShapeDtypeStruct((total, HD), jnp.float32)
    place, table = core.reshape(1), rand_blocks.reshape(-1)
    params = pltpu.CompilerParams(vmem_limit_bytes=40 * 2**20)
    dq_whole, kf, vf, dkf, dvf = pl.pallas_call(
        functools.partial(whole_kernel, chunks, span),
        out_shape=(jax.ShapeDtypeStruct((chunks, many, HD), jnp.bfloat16), held, held, sums, sums),
        in_specs=[smem, smem, vmem, vmem],
        out_specs=(vmem,) * 5,
        compiler_params=params,
        cost_estimate=pl.CostEstimate(flops=14 * 10**9, bytes_accessed=12 * 10**6, transcendentals=0),
    )(place, table, first, sib)
    dq_half, down, dsib = pl.pallas_call(
        functools.partial(half_kernel, chunks, span),
        out_shape=(
            jax.ShapeDtypeStruct((chunks, half, HD), jnp.bfloat16),
            jax.ShapeDtypeStruct((chunks, 2 * span, HD), jnp.float32),
            jax.ShapeDtypeStruct((chunks, 2 * span, HD), jnp.bfloat16),
        ),
        in_specs=[smem, smem] + [vmem] * 5,
        out_specs=(vmem,) * 3,
        scratch_shapes=[pltpu.VMEM((total, HD), jnp.float32)] * 2,
        compiler_params=params,
        cost_estimate=pl.CostEstimate(flops=6 * 10**9, bytes_accessed=12 * 10**6, transcendentals=0),
    )(place, table, second, kf, vf, dkf, dvf)
    part = lax.ppermute(dsib, "head", swap)
    summed = (down + part.astype(jnp.float32)).astype(jnp.bfloat16)
    last = exchange(jnp.concatenate([summed, dq_half, dq_whole], axis=1))

    def flat(cut):
        return cut.transpose(1, 0, 2).reshape(cut.shape[1], chunks * HD)

    got_half, got_whole = last[:, 2 * span : 2 * span + half], last[:, 2 * span + half :]
    dq = jnp.where(
        core == 0,
        jnp.concatenate([got_whole, got_half], axis=1),
        jnp.concatenate([got_half, got_whole], axis=1),
    )
    return flat(dq), flat(last[:, :span]), flat(last[:, span : 2 * span])


def solution(mesh):
    rows = P(("seq", "head"), None)
    seq_count, head_devices = mesh.shape["seq"], mesh.shape["head"]

    def run(query, key, value, grad_out, rand_blocks):
        count = seq_count * head_devices
        heads = query.shape[1] // HD
        span = query.shape[0] // count
        body = on_device
        if head_devices % 2 == 0 and count == 2 * heads and heads % 4 == 0 and 2 * span == 5 * BLOCK:
            body = functools.partial(on_chip_pair, seq_count, head_devices)
        return jax.shard_map(
            body,
            mesh=mesh,
            in_specs=(rows, rows, rows, rows, P()),
            out_specs=(rows, rows, rows),
            check_vma=False,
        )(query, key, value, grad_out, rand_blocks)

    return run
```
